32 devices in a mesh: section: 2 (over x), dp: 4 (over z), tensor: 4 (over y, core).
Axes of the slice: x: 2, y: 2, z: 4, core: 2. Of those that a mesh axis runs over, the one named last changes fastest.
Arguments:
- tokens: bfloat16 [2, 1024, 768], P(None, ('dp', 'tensor')), may hold values from -6 to 6
- cotangent: bfloat16 [2, 1024, 768], P(None, ('dp', 'tensor')), may hold values from -6 to 6
- w_qkv: bfloat16 [2, 3, 768, 768], P('section', None, 'dp', 'tensor'), may hold values from -0.21875 to 0.21875
- w_out: bfloat16 [2, 768, 768], P('section', 'tensor', 'dp'), may hold values from -1.75 to 1.75
- w_gate_up: bfloat16 [2, 2, 768, 3072], P('section', None, 'dp', 'tensor'), may hold values from -0.21875 to 0.21875
- w_down: bfloat16 [2, 3072, 768], P('section', 'tensor', 'dp'), may hold values from -0.109375 to 0.109375
- rel_table: bfloat16 [2, 32, 12], P('section', 'dp', 'tensor'), may hold values from -4 to 4
- gains: bfloat16 [2, 3, 768], P('section', None, ('dp', 'tensor')), may hold values from 0.25 to 1.75
- router: bfloat16 [2, 768, 8], P('section', ('dp', 'tensor')), may hold values from -0.21875 to 0.21875
- w_in: bfloat16 [2, 8, 768, 3072], P('section', 'dp', None, 'tensor'), may hold values from -0.21875 to 0.21875
- w_expert_out: bfloat16 [2, 8, 3072, 768], P('section', 'dp', 'tensor'), may hold values from -0.109375 to 0.109375
- routes: int32 [2, 2, 1024, 2], P('section', None, 'dp'), may hold values from 0 to 7, all different within a row; in each aligned block of 256 rows (0 to 255, 256 to 511, ..., all dimensions but the last counted through in order) at most 80 rows name the same one
Outputs:
- block_out: bfloat16 [2, 2, 1024, 768], P('section', None, ('dp', 'tensor'))
- input_grads: bfloat16 [2, 2, 1024, 768], P('section', None, ('dp', 'tensor'))
- grad_w_qkv: float32 [2, 3, 768, 768], P('section', None, 'dp', 'tensor')
- grad_w_out: float32 [2, 768, 768], P('section', 'tensor', 'dp')
- grad_w_gate_up: float32 [2, 2, 768, 3072], P('section', None, 'dp', 'tensor')
- grad_w_down: float32 [2, 3072, 768], P('section', 'tensor', 'dp')
- grad_rel_table: float32 [2, 32, 12], P('section', 'dp', 'tensor')
- grad_gains: float32 [2, 3, 768], P('section', None, ('dp', 'tensor'))
- grad_router: float32 [2, 768, 8], P('section', ('dp', 'tensor'))
- grad_w_in: float32 [2, 8, 768, 3072], P('section', 'dp', None, 'tensor')
- grad_w_expert_out: float32 [2, 8, 3072, 768], P('section', 'dp', 'tensor')
The draws below stay inside these ranges and needn't reach their ends.
Inputs may be any that keep to these rules, and one draw needn't show every extreme that they name: `routes`: each row names 2 different experts; within each aligned block of 256 rows (one micro-batch's tokens of one dp index) no expert is named more than 80 times.
All inputs are finite; a program needn't handle non-finite values.
Results may differ from the reference program's by a relative error of at most 0.033.
Values may be sent and summed in bfloat16 or wider, within the bound.
A program may use at most 256 MiB of HBM per device.

```python
import math
import jax
import jax.numpy as jnp
import numpy as np
from jax import lax

D = 768
H = 12
HD = 64
FF = 3072
FE = 3072
NB = 32
MAXDIST = 128
TOPK = 2
MICRO = 2
TOK_DP = 256
LENGTH = 1024
TOKENS = 1024
EXPERTS = 8
CAP = 80
N_DP = 4


def level_of(rng, shape, pieces, smallest, top_value):
    def one(axis_at, blocks):
        steps = jax.random.uniform(jax.random.fold_in(jax.random.fold_in(rng, 6), axis_at), (blocks,), jnp.float32, smallest / len(pieces), top_value / len(pieces))
        return jnp.repeat(jnp.exp(steps), shape[axis_at] // blocks).reshape((-1,) + (1,) * (len(shape) - axis_at - 1))

    factor_of = one(*pieces[0])
    for cut in pieces[1:]:
        factor_of = factor_of * one(*cut)
    return factor_of


def deal_out(stream_key, own, number, rows, count, top, most, lean):
    ranking = jax.random.permutation(stream_key, count)
    heavy_load, ordinary = load_shares(count, rows * top, most, lean, True), load_shares(count, rows * top, most, lean, False)
    places = jnp.arange(count)

    def named(lengths, offset_by):
        used = int((lengths > 0).sum())
        fixed = max(1, used // 4)
        shifted = fixed + (places - fixed + offset_by * (used - fixed)) % max(1, count - fixed)
        return jnp.zeros((count,), jnp.int32).at[ranking[jnp.where(places < fixed, places, shifted)]].set(jnp.asarray(lengths, jnp.int32))

    lengths = jnp.where(number % 4 == 0, named(heavy_load, number // 4), named(ordinary, number - number // 4 - 1))
    mixed = jax.random.permutation(jax.random.fold_in(own, 3), count)
    donor, taker = mixed[0:count // 2 * 2:2], mixed[1:count // 2 * 2:2]
    room = jnp.minimum(lengths[donor] - 1, most - lengths[taker]) // 2
    room = jnp.where((donor == ranking[0]) | (taker == ranking[0]) | (lengths[taker] == 0), 0, jnp.maximum(room, 0))
    shifted = jax.random.randint(jax.random.fold_in(own, 4), (count // 2,), 0, 1 << 20) % (room + 1)
    lengths = lengths.at[donor].add(-shifted).at[taker].add(shifted)
    labels = jnp.searchsorted(jnp.cumsum(lengths), jnp.arange(rows * top), side="right").astype(jnp.int32)
    table = labels.reshape(top, rows).T
    table = table[jax.random.permutation(jax.random.fold_in(own, 1), rows)]
    offset_by = jax.random.randint(jax.random.fold_in(own, 2), (rows, 1), 0, top)
    return jnp.take_along_axis(table, (jnp.arange(top)[None, :] + offset_by) % top, axis=1)


def load_shares(amount, total, bound, lean, full):
    loads = [(1 << 20) // math.isqrt(standing ** lean) + 1 for standing in range(1, amount + 1)]
    largest = bound if full else min(bound, max(-(-total // amount), total * loads[0] // sum(loads)))
    least = 1 if total - largest >= amount - 1 else 0
    holding, surplus = [largest] + [least] * (amount - 1), total - largest - least * (amount - 1)
    while surplus > 0:
        movable = [i for i in range(1, amount) if holding[i] < largest] or [i for i in range(1, amount) if holding[i] < bound]
        pool, budget = sum([loads[i] for i in movable]), surplus
        for i in movable:
            addition = min(bound - holding[i], max(1, budget * loads[i] // pool), surplus)
            holding[i] = holding[i] + addition
            surplus = surplus - addition
    return np.array(holding)


def scatter_about(own_key, shape, width, bound, cuts=(), held_as=jnp.bfloat16):
    factor_of = level_of(own_key, shape, cuts, -0.22, 0.18) if cuts else 1.0
    drawn = jax.random.normal(own_key, shape, jnp.float32) * width * factor_of
    return jnp.minimum(jnp.maximum(drawn, -bound), bound).astype(held_as)


def setup_inputs(seed: int = 0) -> dict:
    key_of = jax.random.split(jax.random.key(seed), 13)
    tokens = scatter_about(key_of[0], (MICRO, TOKENS, D), 1.0, 6.0, ((1, 16),))
    cotangent = scatter_about(key_of[1], (MICRO, TOKENS, D), 1.0, 6.0, ((1, 16),))
    w_qkv = scatter_about(key_of[2], (2, 3, D, H * HD), D ** -0.5, 0.21875, ((0, 2), (2, 4), (3, 4)))
    w_out = scatter_about(key_of[3], (2, H * HD, D), (H * HD // 64) ** -0.5, 1.75, ((0, 2), (1, 4), (2, 4)))
    w_gate_up = scatter_about(key_of[4], (2, 2, D, FF), D ** -0.5, 0.21875, ((0, 2), (2, 4), (3, 4)))
    w_down = scatter_about(key_of[5], (2, FF, D), FF ** -0.5, 0.109375, ((0, 2), (1, 4), (2, 4)))
    rel_table = scatter_about(key_of[6], (2, NB, H), 1.0, 4.0, ((0, 2), (1, 4), (2, 4)))
    gains = jnp.clip(1.0 + 0.15 * jax.random.normal(key_of[7], (2, 3, D), jnp.float32), 0.25, 1.75).astype(jnp.bfloat16)
    router = scatter_about(key_of[8], (2, D, EXPERTS), D ** -0.5, 0.21875, ((0, 2), (1, 16)))
    w_in = scatter_about(key_of[9], (2, EXPERTS, D, FE), D ** -0.5, 0.21875, ((0, 2), (1, 4), (3, 4)))
    w_expert_out = scatter_about(key_of[10], (2, EXPERTS, FE, D), FE ** -0.5, 0.109375, ((0, 2), (1, 4), (2, 4)))
    routes_keys = jax.random.split(jax.random.fold_in(key_of[11], 1), 2 * MICRO * TOKENS // TOK_DP)
    routes_turns = jax.random.permutation(jax.random.fold_in(key_of[11], 3), 2 * MICRO * TOKENS // TOK_DP)
    routes = jax.vmap(lambda own, number: deal_out(jax.random.fold_in(key_of[11], 2), own, number, TOK_DP, EXPERTS, TOPK, CAP, 2))(routes_keys, routes_turns).reshape((2, MICRO, TOKENS, TOPK))
    return dict(tokens=tokens, cotangent=cotangent, w_qkv=w_qkv, w_out=w_out, w_gate_up=w_gate_up, w_down=w_down, rel_table=rel_table, gains=gains, router=router, w_in=w_in, w_expert_out=w_expert_out, routes=routes)


highest_precision = lax.Precision.HIGHEST
norm_eps = 1e-06
masked_score = -1000000000.0

@jax.custom_vjp
def low(v):
    return lax.optimization_barrier(v.astype(jnp.bfloat16)).astype(jnp.float32)

@jax.custom_vjp
def low_back(v):
    return v

def low_keep(v):
    return (low(v), None)

def low_pass(kept, grad):
    return (grad,)

def back_keep(v):
    return (v, None)

def back_low(kept, grad):
    return (low(grad),)
low.defvjp(low_keep, low_pass)
low_back.defvjp(back_keep, back_low)

def both_ways(values_in):
    return low(low_back(values_in))

def bucket_edges():
    exact_span = NB // 2
    distance = np.arange(1, 4 * MAXDIST + 1) * 1.0
    log_ratio = np.log(np.maximum(distance, exact_span) / exact_span) / np.log(MAXDIST / exact_span)
    far_bucket = np.minimum(exact_span + np.floor(log_ratio * (NB - exact_span)), NB - 1)
    bucket = np.where(distance < exact_span, distance, far_bucket)
    return [int(distance[np.argmax(bucket >= bucket_no)]) for bucket_no in range(1, NB)]

def relative_bucket(distance):
    bucket = jnp.zeros(distance.shape, jnp.int32)
    for edge_at in bucket_edges():
        bucket = bucket + (distance >= edge_at).astype(jnp.int32)
    return bucket

def norm_rows(hidden_in, gain_row):
    return hidden_in * lax.rsqrt(lax.optimization_barrier(jnp.mean(hidden_in * hidden_in, axis=-1, keepdims=True)) + norm_eps) * gain_row

def gelu_tanh(inputs):
    return jax.nn.gelu(inputs, approximate=True)

def gated(gate_part, up_part):
    return gelu_tanh(gate_part) * up_part

def gate_weights(logits, route_rows):
    chosen = route_rows[:, :, None] == jnp.arange(logits.shape[1], dtype=jnp.int32)[None, None, :]
    picked = lax.optimization_barrier(jnp.sum(jnp.where(chosen, logits[:, None, :], 0.0), axis=2))
    row_max = lax.optimization_barrier(jnp.max(picked, axis=1, keepdims=True))
    raised = jnp.exp(picked - row_max)
    return (raised / lax.optimization_barrier(jnp.sum(raised, axis=1, keepdims=True)), chosen)

def attend_sequence(position_table, queries, key_rows, values):
    position = jnp.arange(LENGTH, dtype=jnp.int32)
    distance = position[:, None] - position[None, :]
    pos_bias = jnp.take(position_table, relative_bucket(distance), axis=0)
    raw_scores = jnp.einsum('qhd,khd->hqk', queries, key_rows, precision=highest_precision) * HD ** (-0.5) + jnp.transpose(pos_bias, (2, 0, 1))
    scores = jnp.where((distance >= 0)[None], low_back(raw_scores), masked_score)
    row_max = lax.optimization_barrier(jnp.max(scores, axis=-1, keepdims=True))
    log_total = row_max + jnp.log(lax.optimization_barrier(jnp.sum(jnp.exp(scores - row_max), axis=-1, keepdims=True)))
    soft = low(jnp.exp(scores - log_total))
    return jnp.einsum('hqk,khd->qhd', soft, values, precision=highest_precision)

def section_block(inputs, weights, route_rows):
    qkv_weight, out_weight, gate_up_weight, down_weight, position_table, gain_rows, router_weight, inner_weight, outer_weight = weights
    residual = low_back(inputs)
    normed = low(norm_rows(residual, gain_rows[0]))
    projected = both_ways(jnp.einsum('td,cdf->ctf', normed, qkv_weight, precision=highest_precision))
    heads_view = projected.reshape(3, TOKENS // LENGTH, LENGTH, H, HD)
    checked = jax.checkpoint(attend_sequence)
    attended = lax.map(lambda parts: checked(position_table, parts[0], parts[1], parts[2]), (heads_view[0], heads_view[1], heads_view[2]))
    attended = both_ways(attended.reshape(TOKENS, H * HD))
    residual1 = residual + low_back(jnp.dot(attended, out_weight, precision=highest_precision))
    normed1 = low(norm_rows(residual1, gain_rows[1]))
    gate_up = low_back(jnp.einsum('td,cdf->ctf', normed1, gate_up_weight, precision=highest_precision))
    hidden = low(gated(gate_up[0], gate_up[1]))
    residual2 = residual1 + low_back(jnp.dot(hidden, down_weight, precision=highest_precision))
    normed2 = low(norm_rows(residual2, gain_rows[2]))
    logits = jnp.dot(normed2, router_weight, precision=highest_precision)
    gate_probs, chosen = gate_weights(logits, route_rows)
    blocks = route_rows.reshape(N_DP, TOK_DP * TOPK)
    one_hot_matrix = (blocks[:, :, None] == jnp.arange(EXPERTS, dtype=jnp.int32)[None, None, :]).astype(jnp.int32)
    before = jnp.cumsum(one_hot_matrix, axis=1) - one_hot_matrix
    slot_place = lax.optimization_barrier(jnp.sum(before * one_hot_matrix, axis=2))
    slot_ids = ((jnp.arange(N_DP, dtype=jnp.int32)[:, None] * EXPERTS + blocks) * CAP + slot_place).reshape(-1)
    copies = jnp.repeat(normed2, TOPK, axis=0)
    buffer = jnp.zeros((N_DP * EXPERTS * CAP, D), jnp.float32).at[slot_ids].set(copies)
    buffer = jnp.transpose(buffer.reshape(N_DP, EXPERTS, CAP, D), (1, 0, 2, 3)).reshape(EXPERTS, N_DP * CAP, D)
    before_act = low_back(jnp.einsum('erd,edf->erf', buffer, inner_weight, precision=highest_precision))
    active = low(gelu_tanh(before_act))
    results = low_back(jnp.einsum('erf,efd->erd', active, outer_weight, precision=highest_precision))
    results = jnp.transpose(results.reshape(EXPERTS, N_DP, CAP, D), (1, 0, 2, 3)).reshape(N_DP * EXPERTS * CAP, D)
    picked = results[slot_ids].reshape(TOKENS, TOPK, D)
    branch = low_back(lax.optimization_barrier(jnp.sum(gate_probs[:, :, None] * picked, axis=1)))
    return low(residual2 + branch)

def reference(tokens, cotangent, w_qkv, w_out, w_gate_up, w_down, rel_table, gains, router, w_in, w_expert_out, routes):
    weights = [tuple((array[section_no].astype(jnp.float32) for array in (w_qkv, w_out, w_gate_up, w_down, rel_table, gains, router, w_in, w_expert_out))) for section_no in range(2)]
    grad_sums = [jax.tree.map(jnp.zeros_like, weights[section_no]) for section_no in range(2)]
    first_out = []
    final_out = []
    first_grad = []
    second_grad = []
    for micro_no in range(MICRO):
        route_first = routes[0, micro_no]
        route_second = routes[1, micro_no]
        middle, back_first = jax.vjp(lambda values_in, params: section_block(values_in, params, route_first), tokens[micro_no].astype(jnp.float32), weights[0])
        result, back_second = jax.vjp(lambda values_in, params: section_block(values_in, params, route_second), middle, weights[1])
        grad_middle, grads_second = back_second(cotangent[micro_no].astype(jnp.float32))
        grad_handed = low(grad_middle)
        grad_input, grads_first = back_first(grad_handed)
        grad_sums[0] = jax.tree.map(jnp.add, grad_sums[0], grads_first)
        grad_sums[1] = jax.tree.map(jnp.add, grad_sums[1], grads_second)
        first_out.append(middle)
        final_out.append(result)
        first_grad.append(grad_input)
        second_grad.append(grad_middle)
    block_out = jnp.stack([jnp.stack(first_out), jnp.stack(final_out)]).astype(jnp.bfloat16)
    input_grads = jnp.stack([jnp.stack(first_grad), jnp.stack(second_grad)]).astype(jnp.bfloat16)
    grad_list = [jnp.stack([grad_sums[0][number], grad_sums[1][number]]) for number in range(9)]
    return (block_out, input_grads, grad_list[0], grad_list[1], grad_list[2], grad_list[3], grad_list[4], grad_list[5], grad_list[6], grad_list[7], grad_list[8])
```

```python
import jax
import jax.numpy as jnp
import numpy as np
from jax import lax
from jax.experimental import pallas as pl
from jax.experimental.pallas import tpu as pltpu
from jax.sharding import PartitionSpec as P

HD = 64
NB = 32
MAXDIST = 128


highest_precision = lax.Precision.HIGHEST
norm_eps = 1e-06
masked_score = -1000000000.0


def from_behind(value, axis, steps):
    count = lax.axis_size(axis)
    first, last = (max(0, -steps), min(count, count - steps))
    return lax.ppermute(value, axis, [(source, source + steps) for source in range(first, last)])


def bucket_edges():
    exact_span = NB // 2
    distance = np.arange(1, 4 * MAXDIST + 1) * 1.0
    log_ratio = np.log(np.maximum(distance, exact_span) / exact_span) / np.log(MAXDIST / exact_span)
    far_bucket = np.minimum(exact_span + np.floor(log_ratio * (NB - exact_span)), NB - 1)
    bucket = np.where(distance < exact_span, distance, far_bucket)
    return [int(distance[np.argmax(bucket >= bucket_no)]) for bucket_no in range(1, NB)]


def relative_bucket(distance):
    bucket = jnp.zeros(distance.shape, jnp.int32)
    for edge_at in bucket_edges():
        bucket = bucket + (distance >= edge_at).astype(jnp.int32)
    return bucket


def norm_rows(hidden_in, gain_row):
    return (
        hidden_in
        * lax.rsqrt(jnp.mean(hidden_in * hidden_in, axis=-1, keepdims=True) + norm_eps)
        * gain_row
    )


def gelu_tanh(inputs):
    return jax.nn.gelu(inputs, approximate=True)


def gated(gate_part, up_part):
    return gelu_tanh(gate_part) * up_part


def gate_weights(logits, route_rows):
    chosen = route_rows[:, :, None] == jnp.arange(logits.shape[1], dtype=jnp.int32)[None, None, :]
    picked = jnp.sum(jnp.where(chosen, logits[:, None, :], 0.0), axis=2)
    row_max = jnp.max(picked, axis=1, keepdims=True)
    raised = jnp.exp(picked - row_max)
    return (raised / jnp.sum(raised, axis=1, keepdims=True), chosen)


VMEM_BYTES = 24 << 20


def whole_specs(count):
    return [pl.BlockSpec(memory_space=pltpu.VMEM)] * count


def push(source, target, sent, landed, device):
    copy = pltpu.make_async_remote_copy(
        src_ref=source,
        dst_ref=target,
        send_sem=sent,
        recv_sem=landed,
        device_id=device,
        device_id_type=pl.DeviceIdType.MESH,
    )
    copy.start()
    return copy


def greet(axis_counts):
    barrier = pltpu.get_barrier_semaphore()
    total = 0
    for axis, count in axis_counts:
        me = lax.axis_index(axis)
        for step in range(1, count):
            pl.semaphore_signal(
                barrier,
                inc=1,
                device_id={axis: lax.rem(me + step, count)},
                device_id_type=pl.DeviceIdType.MESH,
            )
        total += count - 1
    pl.semaphore_wait(barrier, total)


def sum_kernel(count, backward, gather, *refs):
    refs = list(refs)
    part_ref, base_ref = refs[:2]
    del refs[:2]
    if backward:
        value_ref = refs.pop(0)
    if backward or gather:
        gain_ref = refs.pop(0)
    new_ref = refs.pop(0)
    if backward:
        gain_grad_ref = refs.pop(0)
    if gather:
        rows_ref = refs.pop(0)
    out_buf, in_buf, sent, landed = refs[:4]
    me = lax.axis_index("tensor")
    greet([("tensor", count)])
    copies = []
    for step in range(1, count):
        peer = lax.rem(me + step, count)
        out_buf[step - 1] = part_ref[peer].astype(jnp.bfloat16)
        copies.append(
            push(
                out_buf.at[step - 1],
                in_buf.at[step - 1],
                sent.at[step - 1],
                landed.at[step - 1],
                {"tensor": peer},
            )
        )
    total = part_ref[me]
    if not backward:
        total = total + base_ref[...]
    for step in range(1, count):
        copies[step - 1].wait_recv()
        total = total + in_buf[step - 1].astype(jnp.float32)
    if backward:
        value = value_ref[...]
        root = lax.rsqrt(jnp.mean(value * value, axis=-1, keepdims=True) + norm_eps)
        scaled = total * gain_ref[...]
        pull = jnp.mean(scaled * value, axis=-1, keepdims=True)
        gain_grad_ref[...] = jnp.sum(total * (value * root), axis=0, keepdims=True)
        new = base_ref[...] + (root * scaled - value * (root * root * root * pull))
        rounded = new
    else:
        new = total
        if gather:
            rounded = norm_rows(new, gain_ref[...])
    new_ref[...] = new
    if gather:
        sent2, landed2 = refs[4:]
        rows_ref[me] = rounded.astype(jnp.bfloat16)
        for step in range(1, count):
            copies.append(
                push(
                    rows_ref.at[me],
                    rows_ref.at[me],
                    sent2.at[step - 1],
                    landed2.at[step - 1],
                    {"tensor": lax.rem(me + step, count)},
                )
            )
        for copy in copies[count - 1 :]:
            copy.wait_recv()
    for copy in copies:
        copy.wait_send()


def sum_rows(part, base, value=None, gain=None, gather=True):
    backward = value is not None
    count = lax.axis_size("tensor")
    rows, model = base.shape
    args = [part.reshape(count, rows, model), base]
    out_shape = [jax.ShapeDtypeStruct((rows, model), jnp.float32)]
    if backward:
        args.append(value)
        out_shape.append(jax.ShapeDtypeStruct((1, model), jnp.float32))
    if backward or gather:
        args.append(gain[None])
    sems = [pltpu.SemaphoreType.DMA((count - 1,))] * 2
    if gather:
        out_shape.append(jax.ShapeDtypeStruct((count, rows, model), jnp.bfloat16))
        sems = sems * 2
    out = pl.pallas_call(
        lambda *refs: sum_kernel(count, backward, gather, *refs),
        out_shape=out_shape,
        in_specs=whole_specs(len(args)),
        out_specs=whole_specs(len(out_shape)),
        scratch_shapes=[pltpu.VMEM((count - 1, rows, model), jnp.bfloat16)] * 2 + sems,
        compiler_params=pltpu.CompilerParams(
            collective_id=2 * int(backward) + int(gather),
            has_side_effects=True,
            vmem_limit_bytes=VMEM_BYTES,
        ),
    )(*args)
    out = list(out)
    if gather:
        out[-1] = out[-1].reshape(count * rows, model)
    return out


def dispatch_kernel(dp_count, tensor_count, in_ref, out_ref, sent, landed, sent2, landed2):
    me, place = lax.axis_index("dp"), lax.axis_index("tensor")
    high, wide = in_ref.shape[1] // 2, in_ref.shape[2] // 2
    rows = pl.ds(pl.multiple_of((place // 2) * high, 16), high)
    columns = pl.ds(pl.multiple_of((place % 2) * wide, 128), wide)
    greet([("dp", dp_count), ("tensor", tensor_count)])
    first, second = [], []
    for step in range(1, dp_count):
        peer = lax.rem(me + step, dp_count)
        first.append(
            push(
                in_ref.at[peer, rows, columns],
                out_ref.at[me, rows, columns],
                sent.at[step - 1],
                landed.at[step - 1],
                {"dp": peer},
            )
        )
    out_ref[me] = in_ref[me]
    for step in range(1, dp_count):
        first[step - 1].wait_recv()
        source = lax.rem(me + dp_count - step, dp_count)
        for hop in range(1, tensor_count):
            index = (step - 1) * (tensor_count - 1) + hop - 1
            second.append(
                push(
                    out_ref.at[source, rows, columns],
                    out_ref.at[source, rows, columns],
                    sent2.at[index],
                    landed2.at[index],
                    {"tensor": lax.rem(place + hop, tensor_count)},
                )
            )
    for copy in first:
        copy.wait_send()
    for copy in second:
        copy.wait()


def send_rows(part):
    dp_count, tensor_count = lax.axis_size("dp"), lax.axis_size("tensor")
    hops = (dp_count - 1) * (tensor_count - 1)
    return pl.pallas_call(
        lambda *refs: dispatch_kernel(dp_count, tensor_count, *refs),
        out_shape=jax.ShapeDtypeStruct(part.shape, part.dtype),
        in_specs=whole_specs(1),
        out_specs=whole_specs(1)[0],
        scratch_shapes=[pltpu.SemaphoreType.DMA((dp_count - 1,))] * 2
        + [pltpu.SemaphoreType.DMA((hops,))] * 2,
        compiler_params=pltpu.CompilerParams(
            collective_id=4, has_side_effects=True, vmem_limit_bytes=VMEM_BYTES
        ),
    )(part)


def exchange_kernel(dp_count, in_ref, out_ref, sent, landed):
    me = lax.axis_index("dp")
    greet([("dp", dp_count)])
    copies = []
    for step in range(1, dp_count):
        peer = lax.rem(me + step, dp_count)
        copies.append(
            push(
                in_ref.at[peer],
                out_ref.at[me],
                sent.at[step - 1],
                landed.at[step - 1],
                {"dp": peer},
            )
        )
    out_ref[me] = in_ref[me]
    for copy in copies:
        copy.wait()


def send_results(part):
    dp_count = lax.axis_size("dp")
    part = part.astype(jnp.bfloat16)
    return pl.pallas_call(
        lambda *refs: exchange_kernel(dp_count, *refs),
        out_shape=jax.ShapeDtypeStruct(part.shape, part.dtype),
        in_specs=whole_specs(1),
        out_specs=whole_specs(1)[0],
        scratch_shapes=[pltpu.SemaphoreType.DMA((dp_count - 1,))] * 2,
        compiler_params=pltpu.CompilerParams(
            collective_id=5, has_side_effects=True, vmem_limit_bytes=VMEM_BYTES
        ),
    )(part)


def on_device(
    tokens,
    cotangent,
    w_qkv,
    w_out,
    w_gate_up,
    w_down,
    rel_table,
    gains,
    router,
    w_in,
    w_expert_out,
    routes,
):
    dp_count = lax.axis_size("dp")
    tensor_count = lax.axis_size("tensor")
    dp_place = lax.axis_index("dp")
    is_first = lax.axis_index("section") == 0
    micro_count = tokens.shape[0]
    local_rows = tokens.shape[1]
    model = tokens.shape[2]
    tok_dp = local_rows * tensor_count
    seq_span = min(4, dp_count)
    length = tok_dp * seq_span
    expert_count = router.shape[2]
    top_count = routes.shape[3]
    capacity = (5 * tok_dp * top_count + 4 * expert_count - 1) // (4 * expert_count)
    wide = w_qkv.shape[3]
    hidden_wide = w_gate_up.shape[3]
    attn_weight = lax.all_gather(
        jnp.concatenate([w_qkv[0, 0], w_qkv[0, 1], w_qkv[0, 2], w_out[0].T], axis=1),
        "dp",
        axis=0,
        tiled=True,
    )
    mlp_weight = lax.all_gather(
        jnp.concatenate([w_gate_up[0, 0], w_gate_up[0, 1], w_down[0].T], axis=1),
        "dp",
        axis=0,
        tiled=True,
    )
    qkv_weight = attn_weight[:, : 3 * wide]
    out_weight = attn_weight[:, 3 * wide :]
    gate_up_weight = mlp_weight[:, : 2 * hidden_wide]
    down_weight = mlp_weight[:, 2 * hidden_wide :]
    gain_size, small_size = gains[0].size, gains[0].size + router[0].size
    table_rows, heads_here = rel_table.shape[1:]
    packed = jnp.concatenate([gains[0].reshape(-1), router[0].reshape(-1), rel_table[0].reshape(-1)])
    packed_size = packed.size
    packed = jnp.pad(packed, (0, -packed_size % 1024))
    small_all = lax.all_gather(packed, ("dp", "tensor"), axis=0, tiled=False)
    gain_all = (
        small_all[:, :gain_size]
        .reshape(-1, gains.shape[1], gains.shape[2])
        .transpose(1, 0, 2)
        .reshape(gains.shape[1], model)
        .astype(jnp.float32)
    )
    router_all = small_all[:, gain_size:small_size].reshape(model, router.shape[2])
    table_low = lax.dynamic_index_in_dim(
        small_all[:, small_size:packed_size].reshape(dp_count, tensor_count, table_rows, heads_here),
        lax.axis_index("tensor"),
        1,
        keepdims=False,
    ).reshape(dp_count * table_rows, heads_here)
    position_table = table_low.astype(jnp.float32)
    router_wide = router_all.astype(jnp.float32)
    inner_weight = w_in[0]
    outer_weight = w_expert_out[0]
    head_count = position_table.shape[1]
    head_width = head_count * HD
    seq_start = dp_place // seq_span * length
    seq_place = dp_place % seq_span
    own_experts = expert_count // dp_count
    used_rows = own_experts * capacity
    block_rows = -(-used_rows // 32) * 32
    scale = HD ** (-0.5)

    def rows_in(part):
        return lax.all_gather(part, "tensor", axis=0, tiled=True)

    window = min(length, tok_dp + MAXDIST)
    distance = (
        jnp.arange(tok_dp, dtype=jnp.int32)[:, None]
        - (jnp.arange(length, dtype=jnp.int32) - (length - tok_dp))[None, :]
    )
    near_bucket = relative_bucket(distance[:, length - window :])
    one_hot_matrix = (
        near_bucket[None, :, :] == jnp.arange(NB, dtype=jnp.int32)[:, None, None]
    ).astype(jnp.bfloat16)
    nearby_bias = jnp.einsum(
        "vod,vl->lod", one_hot_matrix, table_low, preferred_element_type=jnp.float32
    )
    far_bias = jnp.broadcast_to(
        position_table[NB - 1][:, None, None], (head_count, tok_dp, length - window)
    )
    first_key = (seq_span - 1 - seq_place) * tok_dp
    allowed = (distance >= 0) & (jnp.arange(length, dtype=jnp.int32)[None, :] >= first_key)
    bias = jnp.where(allowed[None], jnp.concatenate([far_bias, nearby_bias], axis=2), masked_score)

    def score_rows(queries, key_rows):
        raw_scores = jnp.einsum(
            "qhd,khd->hqk", queries, key_rows, preferred_element_type=jnp.float32
        )
        return raw_scores * scale + bias

    def slot_matrix(slot_ids):
        slots = jnp.arange(dp_count * block_rows, dtype=jnp.int32)
        return slots[:, None, None] == slot_ids.reshape(tok_dp, top_count).T[None]

    def to_blocks(hits, rows):
        place = jnp.any(hits, axis=1).astype(jnp.bfloat16)
        return jnp.dot(place, rows, preferred_element_type=jnp.float32).astype(jnp.bfloat16)

    def from_blocks(hits, returned):
        flat_rows = returned.reshape(-1, model)
        return jnp.stack(
            [
                jnp.einsum(
                    "st,sd->td",
                    hits[:, top_no].astype(jnp.bfloat16),
                    flat_rows,
                    preferred_element_type=jnp.float32,
                )
                for top_no in range(top_count)
            ],
            axis=1,
        )

    def expert_blocks(rows):
        return rows[:, :used_rows].reshape(dp_count, own_experts, capacity, model)

    def dp_blocks(rows):
        rows = rows.reshape(dp_count, used_rows, model).astype(jnp.bfloat16)
        return jnp.pad(rows, ((0, 0), (0, block_rows - used_rows), (0, 0)))

    def attend_back(queries, pair_rows, log_total, grad_attended):
        key_count = pair_rows.shape[0]
        pairs = pair_rows.reshape(key_count, 2, head_count, HD)
        scores = score_rows(queries, pairs[:, 0])
        soft = jnp.exp(scores - log_total)
        grad_soft = jnp.einsum(
            "qhd,khd->hqk", grad_attended, pairs[:, 1], preferred_element_type=jnp.float32
        )
        inner_sum = jnp.sum(soft * grad_soft, axis=2, keepdims=True)
        grad_scores = (soft * (grad_soft - inner_sum)).astype(jnp.bfloat16)
        nearby_gradient = grad_scores[:, :, length - window :]
        table_gradient = jnp.einsum(
            "ptm,stm->ps", one_hot_matrix, nearby_gradient, preferred_element_type=jnp.float32
        )
        far_sum = jnp.sum(
            grad_scores[:, :, : length - window].astype(jnp.float32), axis=(1, 2)
        )
        table_gradient = table_gradient.at[NB - 1].add(far_sum)
        grad_queries = (
            jnp.einsum("hqk,khd->qhd", grad_scores, pairs[:, 0], preferred_element_type=jnp.float32)
            * scale
        )
        grad_keys = (
            jnp.einsum("hqk,qhd->khd", grad_scores, queries, preferred_element_type=jnp.float32)
            * scale
        )
        grad_values = jnp.einsum(
            "hqk,qhd->khd",
            soft.astype(jnp.bfloat16),
            grad_attended,
            preferred_element_type=jnp.float32,
        )
        grad_pairs = jnp.stack([grad_keys, grad_values], axis=1).reshape(key_count, 2 * head_width)
        return (grad_queries.reshape(tok_dp, head_width), grad_pairs, table_gradient)

    outputs = []
    kept_ticks = []
    arrived_rows = jnp.zeros_like(tokens[0])
    for tick_no in range(micro_count + 1):
        section_input = jnp.where(is_first, tokens[min(tick_no, micro_count - 1)], arrived_rows)
        route_rows = jnp.where(
            is_first, routes[0, min(tick_no, micro_count - 1)], routes[0, max(tick_no - 1, 0)]
        )
        forward_residual = section_input.astype(jnp.float32)
        forward_rows_attn = rows_in(norm_rows(forward_residual, gain_all[0]).astype(jnp.bfloat16))
        projected = jnp.dot(
            forward_rows_attn, qkv_weight, preferred_element_type=jnp.float32
        ).astype(jnp.bfloat16)
        forward_queries = projected[:, :head_width].reshape(tok_dp, head_count, HD)
        everything = lax.all_gather(projected[:, head_width:], "dp", axis=0, tiled=True)
        fetched = lax.dynamic_slice_in_dim(everything, seq_start, length, 0)
        fetched = lax.dynamic_slice_in_dim(
            jnp.concatenate([fetched, fetched]), (seq_place + 1) * tok_dp, length, 0
        )
        attend_pairs = fetched.reshape(fetched.shape[0], 2, head_count, HD)
        attend_scores = score_rows(forward_queries, attend_pairs[:, 0])
        row_max = jnp.max(attend_scores, axis=2, keepdims=True)
        attend_log_total = row_max + jnp.log(
            jnp.sum(jnp.exp(attend_scores - row_max), axis=2, keepdims=True)
        )
        attend_soft = jnp.exp(attend_scores - attend_log_total).astype(jnp.bfloat16)
        attend_attended = jnp.einsum(
            "hqk,khd->qhd", attend_soft, attend_pairs[:, 1], preferred_element_type=jnp.float32
        )
        forward_attended = attend_attended.reshape(tok_dp, head_width).astype(jnp.bfloat16)
        forward_residual1, forward_rows_mlp = sum_rows(
            jnp.einsum(
                "tf,df->td", forward_attended, out_weight, preferred_element_type=jnp.float32
            ),
            forward_residual,
            gain=gain_all[1],
        )
        forward_gate_up = jnp.dot(
            forward_rows_mlp, gate_up_weight, preferred_element_type=jnp.float32
        )
        forward_hidden = gated(
            forward_gate_up[:, :hidden_wide], forward_gate_up[:, hidden_wide:]
        ).astype(jnp.bfloat16)
        forward_residual2, forward_rows_moe = sum_rows(
            jnp.einsum(
                "tf,df->td", forward_hidden, down_weight, preferred_element_type=jnp.float32
            ),
            forward_residual1,
            gain=gain_all[2],
        )
        logits = jnp.dot(forward_rows_moe, router_all, preferred_element_type=jnp.float32)
        forward_gate_probs, forward_chosen = gate_weights(logits, route_rows)
        flat = route_rows.reshape(-1)
        expert_one_hot_matrix = (
            flat[:, None] == jnp.arange(expert_count, dtype=jnp.int32)[None, :]
        ).astype(jnp.bfloat16)
        pair_no = jnp.arange(tok_dp * top_count, dtype=jnp.int32)
        before = jnp.dot(
            (pair_no[:, None] > pair_no[None, :]).astype(jnp.bfloat16),
            expert_one_hot_matrix,
            preferred_element_type=jnp.float32,
        )
        forward_slot_ids = (
            flat // own_experts * block_rows
            + flat % own_experts * capacity
            + jnp.sum(before * expert_one_hot_matrix.astype(jnp.float32), axis=1).astype(jnp.int32)
        )
        forward_hits = slot_matrix(forward_slot_ids)
        forward_arrived = expert_blocks(
            send_rows(
                to_blocks(forward_hits, forward_rows_moe).reshape(dp_count, block_rows, model)
            )
        )
        forward_before_act = jnp.einsum(
            "secd,edf->secf", forward_arrived, inner_weight, preferred_element_type=jnp.float32
        )
        forward_active = gelu_tanh(forward_before_act).astype(jnp.bfloat16)
        results = jnp.einsum(
            "secf,efd->secd", forward_active, outer_weight, preferred_element_type=jnp.float32
        )
        returned = send_results(dp_blocks(results))
        forward_picked_rows = from_blocks(forward_hits, returned)
        residual3 = sum_rows(
            jnp.sum(forward_gate_probs[:, :, None] * forward_picked_rows, axis=1),
            forward_residual2,
            gather=False,
        )[0]
        forward_picked_rows = forward_picked_rows.astype(jnp.bfloat16)
        forward_kept = (
            forward_residual,
            forward_rows_attn,
            forward_queries,
            fetched,
            attend_log_total,
            forward_attended,
            forward_residual1,
            forward_rows_mlp,
            forward_gate_up,
            forward_hidden,
            forward_residual2,
            forward_rows_moe,
            forward_gate_probs,
            forward_chosen,
            forward_slot_ids,
            forward_picked_rows,
            forward_arrived,
            forward_before_act,
            forward_active,
        )
        result = residual3.astype(jnp.bfloat16)
        kept = forward_kept
        outputs.append(result)
        kept_ticks.append(kept)
        if tick_no < micro_count:
            arrived_rows = from_behind(result, "section", 1)
    grad_sums = (
        jnp.zeros(qkv_weight.shape, jnp.float32),
        jnp.zeros(out_weight.shape, jnp.float32),
        jnp.zeros(gate_up_weight.shape, jnp.float32),
        jnp.zeros(down_weight.shape, jnp.float32),
        jnp.zeros(position_table.shape, jnp.float32),
        jnp.zeros(gain_all.shape, jnp.float32),
        jnp.zeros(router_all.shape, jnp.float32),
        jnp.zeros(inner_weight.shape, jnp.float32),
        jnp.zeros(outer_weight.shape, jnp.float32),
    )
    returned_grad = jnp.zeros_like(tokens[0])
    input_list = []
    for tick_no in range(micro_count + 1):
        if tick_no < micro_count:
            outer_cot = cotangent[tick_no]
        else:
            outer_cot = jnp.zeros_like(cotangent[0])
        upstream = jnp.where(is_first, returned_grad, outer_cot)
        kept = jax.tree.map(
            lambda early, late: jnp.where(is_first, early, late),
            kept_ticks[max(tick_no - 1, 0)],
            kept_ticks[min(tick_no + 1, micro_count)],
        )
        (
            residual,
            rows_attn,
            backward_queries,
            backward_pair_rows,
            backward_log_total,
            attended,
            residual1,
            rows_mlp,
            gate_up,
            hidden,
            residual2,
            rows_moe,
            gate_probs,
            chosen,
            slot_ids,
            picked_rows,
            arrived,
            before_act,
            active,
        ) = kept
        grad3 = upstream.astype(jnp.float32)
        rows_grad3 = rows_in(upstream)
        wide_grad3 = rows_grad3.astype(jnp.float32)
        hits = slot_matrix(slot_ids)
        slot_gate = jnp.sum(
            jnp.where(hits, gate_probs.T[None], 0.0), axis=(1, 2)
        )
        slot_place = jnp.any(hits, axis=1).astype(jnp.bfloat16)
        outgoing = (
            jnp.dot(slot_place, rows_grad3, preferred_element_type=jnp.float32)
            * slot_gate[:, None]
        ).astype(jnp.bfloat16)
        grad_results = expert_blocks(send_rows(outgoing.reshape(dp_count, block_rows, model)))
        grad_gate = jnp.sum(wide_grad3[:, None, :] * picked_rows.astype(jnp.float32), axis=2)
        grad_active = jnp.einsum(
            "secd,efd->secf", grad_results, outer_weight, preferred_element_type=jnp.float32
        )
        outer_grad = jnp.einsum(
            "secf,secd->efd", active, grad_results, preferred_element_type=jnp.float32
        )
        gelu_back = jax.vjp(gelu_tanh, before_act)[1]
        grad_before = gelu_back(grad_active)[0].astype(jnp.bfloat16)
        inner_grad = jnp.einsum(
            "secd,secf->edf", arrived, grad_before, preferred_element_type=jnp.float32
        )
        grad_arrived = jnp.einsum(
            "secf,edf->secd", grad_before, inner_weight, preferred_element_type=jnp.float32
        )
        grad_back = send_results(dp_blocks(grad_arrived))
        grad_copies = jnp.einsum(
            "st,sd->td",
            slot_place,
            grad_back.reshape(-1, model),
            preferred_element_type=jnp.float32,
        )
        grad_picked = gate_probs * (
            grad_gate - jnp.sum(gate_probs * grad_gate, axis=1, keepdims=True)
        )
        grad_logits = jnp.sum(jnp.where(chosen, grad_picked[:, :, None], 0.0), axis=1)
        router_grad = jnp.dot(
            rows_moe.astype(jnp.float32).T, grad_logits, precision=highest_precision
        )
        grad_moe_rows = grad_copies + jnp.dot(
            grad_logits, router_wide.T, precision=highest_precision
        )
        grad2, gain_grad2, rows_grad2 = sum_rows(
            grad_moe_rows, grad3, residual2, gain_all[2]
        )
        grad_hidden = jnp.dot(rows_grad2, down_weight, preferred_element_type=jnp.float32)
        down_grad = jnp.einsum("td,tf->df", rows_grad2, hidden, preferred_element_type=jnp.float32)
        gated_back = jax.vjp(gated, gate_up[:, :hidden_wide], gate_up[:, hidden_wide:])[1]
        grad_gate_up = jnp.concatenate(gated_back(grad_hidden), axis=1).astype(jnp.bfloat16)
        gate_up_grad = jnp.einsum(
            "td,tf->df", rows_mlp, grad_gate_up, preferred_element_type=jnp.float32
        )
        grad_mid = jnp.einsum(
            "tf,df->td", grad_gate_up, gate_up_weight, preferred_element_type=jnp.float32
        )
        grad1, gain_grad1, rows_grad1 = sum_rows(grad_mid, grad2, residual1, gain_all[1])
        backward_grad_attended = jnp.dot(
            rows_grad1, out_weight, preferred_element_type=jnp.float32
        ).astype(jnp.bfloat16)
        output_gradient = jnp.einsum(
            "td,tf->df", rows_grad1, attended, preferred_element_type=jnp.float32
        )
        backward_grad_queries, backward_grad_pairs, backward_table_gradient = attend_back(
            backward_queries,
            backward_pair_rows,
            backward_log_total,
            backward_grad_attended.reshape(tok_dp, head_count, HD),
        )
        low_pairs = backward_grad_pairs.astype(jnp.bfloat16)
        spread_rows = lax.dynamic_slice_in_dim(
            jnp.concatenate([low_pairs, low_pairs]), first_key, length, 0
        )
        if dp_count > seq_span:
            spread_rows = lax.dynamic_update_slice_in_dim(
                jnp.zeros((dp_count * tok_dp, 2 * head_width), jnp.bfloat16),
                spread_rows,
                seq_start,
                0,
            )
        own_rows = lax.psum_scatter(spread_rows, "dp", scatter_dimension=0, tiled=True)
        grad_project = jnp.concatenate(
            [backward_grad_queries.astype(jnp.bfloat16), own_rows], axis=1
        )
        qkv_grad = jnp.einsum(
            "td,tf->df", rows_attn, grad_project, preferred_element_type=jnp.float32
        )
        grad0, gain_grad0 = sum_rows(
            jnp.einsum(
                "tf,df->td", grad_project, qkv_weight, preferred_element_type=jnp.float32
            ),
            grad1,
            residual,
            gain_all[0],
            gather=False,
        )
        gain_grad = jnp.concatenate([gain_grad0, gain_grad1, gain_grad2])
        step_grads = (
            qkv_grad,
            output_gradient,
            gate_up_grad,
            down_grad,
            backward_table_gradient,
            gain_grad,
            router_grad,
            inner_grad,
            outer_grad,
        )
        grad_input, step_grads = (grad0.astype(jnp.bfloat16), step_grads)
        grad_sums = jax.tree.map(jnp.add, grad_sums, step_grads)
        input_list.append(grad_input)
        if tick_no < micro_count:
            returned_grad = from_behind(grad_input, "section", -1)
    block_out = jnp.stack(
        [
            jnp.where(is_first, outputs[micro_no], outputs[micro_no + 1])
            for micro_no in range(micro_count)
        ]
    )[None]
    input_grads = jnp.stack(
        [
            jnp.where(is_first, input_list[micro_no + 1], input_list[micro_no])
            for micro_no in range(micro_count)
        ]
    )[None]
    mlp_grads = lax.psum_scatter(
        jnp.concatenate([grad_sums[2], grad_sums[3]], axis=1).astype(jnp.bfloat16),
        "dp",
        scatter_dimension=0,
        tiled=True,
    ).astype(jnp.float32)
    attn_grads = lax.psum_scatter(
        jnp.concatenate([grad_sums[0], grad_sums[1]], axis=1).astype(jnp.bfloat16),
        "dp",
        scatter_dimension=0,
        tiled=True,
    ).astype(jnp.float32)
    devices = dp_count * tensor_count
    is_mine = jnp.arange(tensor_count) == lax.axis_index("tensor")
    table_shares = jnp.where(
        is_mine[None, :, None], grad_sums[4].reshape(dp_count, 1, table_rows * heads_here), 0.0
    )
    small = jnp.concatenate(
        [
            grad_sums[5]
            .reshape(gains.shape[1], devices, gains.shape[2])
            .transpose(1, 0, 2)
            .reshape(devices, -1),
            grad_sums[6].reshape(devices, -1),
            table_shares.reshape(devices, -1),
        ],
        axis=1,
    )
    small = jnp.pad(small, ((0, 0), (0, -packed_size % 1024)))
    small = lax.psum_scatter(small, ("dp", "tensor"), scatter_dimension=0, tiled=False)
    return (
        block_out,
        input_grads,
        jnp.stack([attn_grads[:, part * wide : (part + 1) * wide] for part in range(3)])[None],
        attn_grads[:, 3 * wide :].T[None],
        jnp.stack([mlp_grads[:, :hidden_wide], mlp_grads[:, hidden_wide : 2 * hidden_wide]])[None],
        mlp_grads[:, 2 * hidden_wide :].T[None],
        small[small_size:packed_size].reshape(1, table_rows, heads_here),
        small[:gain_size].reshape(1, gains.shape[1], gains.shape[2]),
        small[gain_size:small_size].reshape(1, router.shape[1], router.shape[2]),
        grad_sums[7][None],
        grad_sums[8][None],
    )


def solution(mesh):
    placed = (
        P(None, ("dp", "tensor"), None),
        P(None, ("dp", "tensor"), None),
        P("section", None, "dp", "tensor"),
        P("section", "tensor", "dp"),
        P("section", None, "dp", "tensor"),
        P("section", "tensor", "dp"),
        P("section", "dp", "tensor"),
        P("section", None, ("dp", "tensor")),
        P("section", ("dp", "tensor"), None),
        P("section", "dp", None, "tensor"),
        P("section", "dp", "tensor", None),
        P("section", None, "dp", None),
    )
    return jax.shard_map(
        on_device,
        mesh=mesh,
        in_specs=placed,
        out_specs=(
            P("section", None, ("dp", "tensor"), None),
            P("section", None, ("dp", "tensor"), None),
            P("section", None, "dp", "tensor"),
            P("section", "tensor", "dp"),
            P("section", None, "dp", "tensor"),
            P("section", "tensor", "dp"),
            P("section", "dp", "tensor"),
            P("section", None, ("dp", "tensor")),
            P("section", ("dp", "tensor"), None),
            P("section", "dp", None, "tensor"),
            P("section", "dp", "tensor", None),
        ),
        check_vma=False,
    )
```
